32 devices in a mesh: pipe: 2 (over y), dp: 4 (over z), expert: 4 (over x, core).
Axes of the slice: x: 2, y: 2, z: 4, core: 2. Of those that a mesh axis runs over, the one named last changes fastest.
Arguments:
- input_grad: bfloat16 [2, 2048, 2048], P('pipe', ('dp', 'expert')), may hold values from -0.1796875 to 0.1796875
- gate_prob: float32 [2, 2048], P('pipe', ('dp', 'expert')), may hold values from 0.2 to 1
- expert_route: int32 [2, 2048, 1], P('pipe', ('dp', 'expert')), may hold values from 0 to 1; in each aligned block of 128 rows (0 to 127, 128 to 255, ..., all dimensions but the last counted through in order) at most 128 rows name the same one
- saved_hidden: bfloat16 [2, 4, 4, 128, 5632], P('pipe', 'dp', None, None, 'expert'), may hold values from -6 to 6
Outputs:
- down_grad: bfloat16 [2, 2048, 5632], P('pipe', 'dp', 'expert')
The draws below stay inside these ranges and needn't reach their ends.
Inputs may be any that keep to these rules, and one draw needn't show every extreme that they name: `expert_route`: among the 128 tokens of one index of dp and expert no expert is named more than 128 times, and in every draw some expert is named exactly 128 times by some device's tokens.
All inputs are finite; a program needn't handle non-finite values.
Results may differ from the reference program's by a relative error of at most 0.014.
Values may be sent and summed in bfloat16 or wider, within the bound.
No kernel may reach another device: no remote copies, remote signals or barrier semaphores. Data moves between devices by JAX's collectives and lax.ppermute only.
A program may use at most 64 MiB of HBM per device.

```python
import math
import jax
import jax.numpy as jnp
import numpy as np
from jax import lax

D = 2048
HW = 2816
SHARDS = 2
TOK = 128
EF = 2
CAP = 128
TOKENS = 2048
N_PIPE = 2
N_DP = 4
N_EXPERT = 4


def raised(values, own_key, source, target, parts, factor):
    owner, partner = [(jnp.arange(values.shape[axis_at]) // (values.shape[axis_at] // parts)).reshape([-1 if axis == axis_at else 1 for axis in range(values.ndim)]) for axis_at in (source, target)]
    chosen = jax.random.permutation(own_key, parts)[partner]
    strong = (owner == chosen) | (owner == (partner + parts // 2) % parts)
    return jnp.where(strong, factor * values, values)


def steps_of(rng, extent, cuts, low, top_value):
    level, own = 1.0, jax.random.fold_in(rng, 6)
    for dim, shards_of in cuts:
        heights = jnp.exp(jax.random.uniform(jax.random.fold_in(own, dim), (shards_of,), jnp.float32, low / len(cuts), top_value / len(cuts)))
        level = level * jnp.repeat(heights, extent[dim] // shards_of).reshape([-1 if axis == dim else 1 for axis in range(len(extent))])
    return level


def deal_out(rng, own, number, rows, amount, top, limit, slope):
    ranking = jax.random.permutation(rng, amount)
    crowded, usual = portions_of(amount, rows * top, limit, slope, True), portions_of(amount, rows * top, limit, slope, False)
    places = jnp.arange(amount)

    def named(lengths, rotation):
        used = int((lengths > 0).sum())
        fixed = max(1, used // 4)
        passed = fixed + (places - fixed + rotation * (used - fixed)) % max(1, amount - fixed)
        return jnp.zeros((amount,), jnp.int32).at[ranking[jnp.where(places < fixed, places, passed)]].set(jnp.asarray(lengths, jnp.int32))

    lengths = jnp.where(number % 4 == 0, named(crowded, number // 4), named(usual, number - number // 4 - 1))
    mixed = jax.random.permutation(jax.random.fold_in(own, 3), amount)
    source_of, receiver = mixed[0:amount // 2 * 2:2], mixed[1:amount // 2 * 2:2]
    slack = jnp.minimum(lengths[source_of] - 1, limit - lengths[receiver]) // 2
    slack = jnp.where((source_of == ranking[0]) | (receiver == ranking[0]) | (lengths[receiver] == 0), 0, jnp.maximum(slack, 0))
    passed = jax.random.randint(jax.random.fold_in(own, 4), (amount // 2,), 0, 1 << 20) % (slack + 1)
    lengths = lengths.at[source_of].add(-passed).at[receiver].add(passed)
    members = jnp.searchsorted(jnp.cumsum(lengths), jnp.arange(rows * top), side="right").astype(jnp.int32)
    grid = members.reshape(top, rows).T
    grid = grid[jax.random.permutation(jax.random.fold_in(own, 1), rows)]
    rotation = jax.random.randint(jax.random.fold_in(own, 2), (rows, 1), 0, top)
    return jnp.take_along_axis(grid, (jnp.arange(top)[None, :] + rotation) % top, axis=1)


def portions_of(count, total, most, lean, full):
    loads = [(1 << 20) // math.isqrt(grade ** lean) + 1 for grade in range(1, count + 1)]
    largest = most if full else min(most, max(-(-total // count), total * loads[0] // sum(loads)))
    least = 1 if total - largest >= count - 1 else 0
    counts, spare = [largest] + [least] * (count - 1), total - largest - least * (count - 1)
    while spare > 0:
        candidates = [i for i in range(1, count) if counts[i] < largest] or [i for i in range(1, count) if counts[i] < most]
        pool, budget = sum([loads[i] for i in candidates]), spare
        for i in candidates:
            addition = min(most - counts[i], max(1, budget * loads[i] // pool), spare)
            counts[i] = counts[i] + addition
            spare = spare - addition
    return np.array(counts)


def scatter_about(rng, dims, deviation, most, split=(), kind=jnp.bfloat16):
    drawn = deviation * jax.random.normal(rng, dims, jnp.float32)
    if split:
        drawn = drawn * steps_of(rng, dims, split, -0.22, 0.18)
    return jnp.clip(drawn, -most, most).astype(kind)


def noise_with(own_key, dims, width, bound, shards, heavy, kind=jnp.bfloat16):
    values = width * jax.random.normal(own_key, dims, jnp.float32)
    if shards:
        values = values * steps_of(own_key, dims, shards, -0.22, 0.18)
    return jnp.clip(raised(values, jax.random.fold_in(own_key, 3), *heavy), -bound, bound).astype(kind)


def setup_inputs(seed: int = 0) -> dict:
    keys = jax.random.split(jax.random.key(seed), 5)
    input_grad = noise_with(keys[0], (N_PIPE, TOKENS, D), 0.03, 0.1796875, ((0, 2), (1, 16)), (1, 2, 16, 2.0))
    gate_prob = jnp.clip(0.2 + 0.8 * jax.random.uniform(keys[1], (N_PIPE, TOKENS), jnp.float32) ** steps_of(keys[1], (N_PIPE, TOKENS), ((0, 2), (1, 16)), -0.2, 0.2), 0.2, 1.0)
    expert_route_keys = jax.random.split(jax.random.fold_in(keys[2], 1), N_PIPE * TOKENS // TOK)
    expert_route_turns = jax.random.permutation(jax.random.fold_in(keys[2], 3), N_PIPE * TOKENS // TOK)
    expert_route = jax.vmap(lambda own, number: deal_out(jax.random.fold_in(keys[2], 2), own, number, TOK, EF, 1, CAP, 2))(expert_route_keys, expert_route_turns).reshape((N_PIPE, TOKENS, 1))
    saved_hidden = scatter_about(keys[3], (N_PIPE, N_DP, N_EXPERT, CAP, EF * HW), 1.0, 6.0, ((0, 2), (1, 4), (4, 4)))
    return dict(input_grad=input_grad, gate_prob=gate_prob, expert_route=expert_route, saved_hidden=saved_hidden)


def slot_table(routes, flight_count, capacity):
    one_hot = (routes[..., None] == jnp.arange(flight_count, dtype=jnp.int32)).astype(jnp.int32)
    earlier = jnp.cumsum(one_hot, axis=-2) - one_hot
    position = jnp.sum(earlier * one_hot, axis=-1)
    in_slot = (position[..., None] == jnp.arange(capacity, dtype=jnp.int32)).astype(jnp.int32)
    return one_hot[..., :, None] * in_slot[..., None, :]


def reference(input_grad, gate_prob, expert_route, saved_hidden):
    flight_count = N_EXPERT // SHARDS
    grad_next = jnp.roll(input_grad, -1, axis=0)

    def one_section(pieces):
        section_grad, section_prob, section_route, section_hidden = pieces
        grad_rows = section_grad.reshape(N_DP, N_EXPERT, TOK, D)
        probs = section_prob.reshape(N_DP, N_EXPERT, TOK)
        routes = section_route[:, 0].reshape(N_DP, N_EXPERT, TOK)
        scaled = (probs[..., None] * grad_rows.astype(jnp.float32)).astype(jnp.bfloat16)
        slot_hit = slot_table(routes, flight_count, CAP).astype(jnp.float32)
        dispatched = jnp.einsum("ritec,ritd->riecd", slot_hit, scaled.astype(jnp.float32)).astype(jnp.bfloat16)
        hidden = section_hidden.reshape(N_DP, N_EXPERT, CAP, flight_count, HW)

        def one_expert(expert_index):
            rows_expert = lax.dynamic_index_in_dim(dispatched, expert_index, 2, keepdims=False)
            hidden_expert = lax.dynamic_index_in_dim(hidden, expert_index, 3, keepdims=False)
            partial_value = jnp.einsum("ricd,rich->rdh", rows_expert.astype(jnp.float32), hidden_expert.astype(jnp.float32))
            partial_value = lax.optimization_barrier(partial_value.astype(jnp.bfloat16)).astype(jnp.float32)
            return jnp.sum(partial_value, axis=0).astype(jnp.bfloat16)

        grads = lax.map(one_expert, jnp.arange(flight_count, dtype=jnp.int32))
        return jnp.transpose(grads, (1, 0, 2)).reshape(D, flight_count * HW)

    return lax.map(one_section, (grad_next, gate_prob, expert_route, saved_hidden))
```

```python
import jax
import jax.numpy as jnp
from jax import lax
from jax.sharding import PartitionSpec as P


def shifted(value, axis, steps):
    count = lax.axis_size(axis)
    pairs = [(source, (source + steps) % count) for source in range(count)]
    return lax.ppermute(value, axis, pairs)


def crossed(value, axis, mask):
    pairs = [(source, source ^ mask) for source in range(lax.axis_size(axis))]
    return lax.ppermute(value, axis, pairs)


def general_body(input_grad, gate_prob, expert_route, saved_hidden):
    grad_rows = shifted(input_grad, "pipe", -1)[0]
    flight_count = lax.axis_size("expert") // 2
    capacity = saved_hidden.shape[3]
    token_count = grad_rows.shape[0]
    model_width = grad_rows.shape[1]
    routes = expert_route[0, :, 0]
    one_hot = (routes[:, None] == jnp.arange(flight_count, dtype=jnp.int32)[None, :]).astype(
        jnp.float32
    )
    row_ids = lax.broadcasted_iota(jnp.int32, (token_count, token_count), 0)
    column_ids = lax.broadcasted_iota(jnp.int32, (token_count, token_count), 1)
    earlier_mask = (column_ids < row_ids).astype(jnp.float32)
    before = jnp.dot(earlier_mask, one_hot, precision=lax.Precision.HIGHEST)
    position = jnp.sum(before * one_hot, axis=1)
    slot_values = jnp.arange(capacity, dtype=jnp.float32)
    slot_hit = one_hot[:, :, None] * (position[:, None, None] == slot_values[None, None, :]).astype(
        jnp.float32
    )
    scaled = (gate_prob[0][:, None] * grad_rows.astype(jnp.float32)).astype(jnp.bfloat16)
    outgoing = jnp.einsum(
        "tec,td->ecd", slot_hit.astype(jnp.bfloat16), scaled, preferred_element_type=jnp.float32
    ).astype(jnp.bfloat16)
    halves = outgoing.reshape(2 * flight_count, capacity // 2, model_width)
    owned_rows = lax.all_to_all(halves, "expert", split_axis=0, concat_axis=0, tiled=True)
    partner_rows = crossed(owned_rows, "expert", 1)
    parity = lax.axis_index("expert") % 2
    first_half = jnp.where(parity == 0, owned_rows, partner_rows)
    second_half = jnp.where(parity == 0, partner_rows, owned_rows)
    received = jnp.concatenate([first_half, second_half], axis=1)
    source_count = received.shape[0]
    flat_rows = received.reshape(source_count * capacity, model_width)
    hidden = saved_hidden.reshape(source_count * capacity, saved_hidden.shape[4])
    summed = lax.psum_scatter(
        lax.dot_general(
            flat_rows, hidden, (((0,), (0,)), ((), ())), preferred_element_type=jnp.float32
        ).astype(jnp.bfloat16),
        "dp",
        scatter_dimension=0,
        tiled=True,
    )
    return summed[None]


def column_cuts(width, parts):
    tiles = width // 128
    edges = [128 * ((tiles * part) // parts) for part in range(parts)] + [width]
    return list(zip(edges[:-1], edges[1:]))


def pair_body(input_grad, gate_prob, expert_route, saved_hidden):
    bf16, f32 = jnp.bfloat16, jnp.float32
    replicas, shards = lax.axis_size("dp"), lax.axis_size("expert")
    replica, shard = lax.axis_index("dp"), lax.axis_index("expert")
    expert, core = shard // 2, shard % 2
    tokens, width = input_grad.shape[1], input_grad.shape[2]
    half = tokens // 2
    sources, hidden_width = saved_hidden.shape[2], saved_hidden.shape[4]
    hidden = saved_hidden[0, 0]
    inner = (replica == 1) | (replica == 2)
    cuts = column_cuts(hidden_width, 4)

    grad_rows = shifted(input_grad, "pipe", -1)[0]
    spilled = [crossed(hidden[:, half:, low:high], "expert", 2) for low, high in cuts]

    routes = expert_route[0, :, 0]
    mine = jnp.sum((routes == 0).astype(f32))
    lane = lax.broadcasted_iota(jnp.int32, (8, 128), 1)
    tally = jnp.where(lane == replica * shards + shard, mine, 0.0)
    tally = tally + crossed(tally, "expert", 1) + crossed(tally, "expert", 2) + crossed(tally, "expert", 3)
    counts = tally + crossed(tally, "dp", 1) + crossed(tally, "dp", 2) + crossed(tally, "dp", 3)

    def held(table, owner):
        wanted = lane[:1, :, None] * 0 + lax.broadcasted_iota(jnp.int32, (1, 128, sources), 2)
        hit = lane[:1, :, None] == owner * shards + wanted
        zeros = jnp.sum(jnp.where(hit, table[:1, :, None], 0.0), axis=1)[0]
        own = jnp.where(expert == 0, zeros, tokens - zeros)
        return jnp.arange(half, dtype=f32)[None, :] < own[:, None]

    keep = held(tally, replica)
    mirror = (jnp.arange(half)[:, None] + jnp.arange(half)[None, :] == half - 1).astype(bf16)
    blocks = []
    for (low, high), spill in zip(cuts, spilled):
        turned = jnp.einsum("cs,isk->ick", mirror, spill, preferred_element_type=f32).astype(bf16)
        packed = jnp.where(keep[:, :, None], hidden[:, :half, low:high], turned)
        packed = packed.reshape(sources * half, high - low)
        first = crossed(packed, "dp", 1)
        near = lax.ppermute(packed, "dp", [(1, 2), (2, 1)])
        far = lax.ppermute(packed, "dp", [(0, 2), (3, 1)])
        near_out = lax.ppermute(near, "dp", [(2, 3), (1, 0)])
        far_out = lax.ppermute(far, "dp", [(2, 3), (1, 0)])
        blocks.append(
            jnp.concatenate(
                [packed, first, jnp.where(inner, far, near_out), jnp.where(inner, near, far_out)], axis=0
            )
        )

    index = lax.broadcasted_iota(jnp.int32, (tokens, tokens), 0)
    other = lax.broadcasted_iota(jnp.int32, (tokens, tokens), 1)
    earlier = (index < other) & (routes[:, None] == routes[None, :])
    slot = jnp.sum(earlier.astype(jnp.int32), axis=0)
    place = jnp.where(routes == 0, slot, tokens - 1 - slot)
    place = jnp.where(place < half, place, tokens + half - 1 - place)
    pick = (index == place[None, :]).astype(bf16)
    scaled = (gate_prob[0][:, None] * grad_rows.astype(f32)).astype(bf16)
    rows = jnp.dot(pick, scaled, preferred_element_type=f32).astype(bf16)
    part = width // replicas // 2
    pieces = rows.reshape(2, half, replicas, 2, part).transpose(0, 3, 2, 1, 4)
    pieces = pieces.reshape(shards, replicas, half, part)

    def piece(values, at):
        return lax.dynamic_index_in_dim(values, at, 0, keepdims=False)

    got = [piece(pieces, shard)] + [
        crossed(piece(pieces, shard ^ mask), "expert", mask) for mask in (1, 2, 3)
    ]
    got = jnp.stack(got)
    ordered = jnp.stack([piece(got, shard ^ source) for source in range(sources)], axis=1)
    arrived = [piece(ordered, replica)] + [
        crossed(piece(ordered, replica ^ mask), "dp", mask) for mask in (1, 2, 3)
    ]
    arrived = jnp.stack(arrived)
    swapped = crossed(arrived, "expert", 1)
    left = jnp.where(core == 0, arrived, swapped)
    right = jnp.where(core == 0, swapped, arrived)
    grads = jnp.concatenate([left, right], axis=3)
    ours = jnp.stack([held(counts, replica ^ mask) for mask in range(replicas)])[..., None]
    both = jnp.concatenate([jnp.where(ours, grads, 0), jnp.where(ours, 0, grads)], axis=3)
    both = both.reshape(replicas * sources * half, 4 * part)

    outs = []
    for block in blocks:
        total = lax.dot_general(both, block, (((0,), (0,)), ((), ())), preferred_element_type=f32)
        theirs = crossed(total[2 * part :].astype(bf16), "expert", 2)
        outs.append((total[: 2 * part] + theirs.astype(f32)).astype(bf16))
    return jnp.concatenate(outs, axis=1)[None]


def solution(mesh):
    in_specs = (
        P("pipe", ("dp", "expert"), None),
        P("pipe", ("dp", "expert")),
        P("pipe", ("dp", "expert"), None),
        P("pipe", "dp", None, None, "expert"),
    )
    out_specs = P("pipe", "dp", "expert")

    def run(input_grad, gate_prob, expert_route, saved_hidden):
        devices = mesh.shape["dp"] * mesh.shape["expert"]
        tokens = input_grad.shape[1] // devices
        pairs = mesh.shape["expert"] == 4 and mesh.shape["dp"] == 4
        body = pair_body if pairs and saved_hidden.shape[3] == tokens else general_body
        return jax.shard_map(body, mesh=mesh, in_specs=in_specs, out_specs=out_specs, check_vma=False)(
            input_grad, gate_prob, expert_route, saved_hidden
        )

    return run
```

```python
import jax
import jax.numpy as jnp
from jax import lax
from jax.sharding import PartitionSpec as P

CUTS = (2, 3, 3, 3)
GROUPS = (1, 1, 1, 1)
ORDER = {
    "F2": ("F0",),
    "F3": ("F1",),
    "M2": ("M0",),
    "M3": ("M2",),
    "N1": ("G", "H"),
    "N2": ("G", "H"),
    "N3": ("G", "H"),
    "P1": ("A1",),
    "S1": ("sent",),
    "S2": ("X",),
    "S3": ("X",),
    "T0": ("upper0",),
    "T1": ("T0", "sent", "upper1"),
    "T2": ("own0",),
    "T3": ("share1", "share2", "share3"),
    "couple0": ("T3",),
    "own0": ("T1",),
    "own1": ("T3",),
    "pair": ("T2",),
    "scaled": ("T0",),
}


def shifted(value, axis, steps):
    count = lax.axis_size(axis)
    pairs = [(source, (source + steps) % count) for source in range(count)]
    return lax.ppermute(value, axis, pairs)


def crossed(value, axis, mask):
    pairs = [(source, source ^ mask) for source in range(lax.axis_size(axis))]
    return lax.ppermute(value, axis, pairs)


def general_body(input_grad, gate_prob, expert_route, saved_hidden):
    grad_rows = shifted(input_grad, "pipe", -1)[0]
    flight_count = lax.axis_size("expert") // 2
    capacity = saved_hidden.shape[3]
    token_count = grad_rows.shape[0]
    model_width = grad_rows.shape[1]
    routes = expert_route[0, :, 0]
    one_hot = (routes[:, None] == jnp.arange(flight_count, dtype=jnp.int32)[None, :]).astype(
        jnp.float32
    )
    row_ids = lax.broadcasted_iota(jnp.int32, (token_count, token_count), 0)
    column_ids = lax.broadcasted_iota(jnp.int32, (token_count, token_count), 1)
    earlier_mask = (column_ids < row_ids).astype(jnp.float32)
    before = jnp.dot(earlier_mask, one_hot, precision=lax.Precision.HIGHEST)
    position = jnp.sum(before * one_hot, axis=1)
    slot_values = jnp.arange(capacity, dtype=jnp.float32)
    slot_hit = one_hot[:, :, None] * (position[:, None, None] == slot_values[None, None, :]).astype(
        jnp.float32
    )
    scaled = (gate_prob[0][:, None] * grad_rows.astype(jnp.float32)).astype(jnp.bfloat16)
    outgoing = jnp.einsum(
        "tec,td->ecd", slot_hit.astype(jnp.bfloat16), scaled, preferred_element_type=jnp.float32
    ).astype(jnp.bfloat16)
    halves = outgoing.reshape(2 * flight_count, capacity // 2, model_width)
    owned_rows = lax.all_to_all(halves, "expert", split_axis=0, concat_axis=0, tiled=True)
    partner_rows = crossed(owned_rows, "expert", 1)
    parity = lax.axis_index("expert") % 2
    first_half = jnp.where(parity == 0, owned_rows, partner_rows)
    second_half = jnp.where(parity == 0, partner_rows, owned_rows)
    received = jnp.concatenate([first_half, second_half], axis=1)
    source_count = received.shape[0]
    flat_rows = received.reshape(source_count * capacity, model_width)
    hidden = saved_hidden.reshape(source_count * capacity, saved_hidden.shape[4])
    summed = lax.psum_scatter(
        lax.dot_general(
            flat_rows, hidden, (((0,), (0,)), ((), ())), preferred_element_type=jnp.float32
        ).astype(jnp.bfloat16),
        "dp",
        scatter_dimension=0,
        tiled=True,
    )
    return summed[None]


def column_cuts(width, weights):
    tiles, whole = width // 128, sum(weights)
    edges = [128 * ((tiles * sum(weights[:part])) // whole) for part in range(len(weights))] + [width]
    return list(zip(edges[:-1], edges[1:]))


def after(value, *others):
    return lax.optimization_barrier((value, *others))[0]


class Plan:
    def __init__(self, input_grad, gate_prob, expert_route, saved_hidden):
        self.made = {}
        self.args = input_grad, gate_prob, expert_route
        self.replica, self.shard = lax.axis_index("dp"), lax.axis_index("expert")
        self.replicas, self.shards = lax.axis_size("dp"), lax.axis_size("expert")
        self.expert, self.core = self.shard // 2, self.shard % 2
        self.inner = (self.replica == 1) | (self.replica == 2)
        self.tokens, self.width = input_grad.shape[1:]
        self.half = self.tokens // 2
        self.hidden = saved_hidden[0, 0]
        self.sources, self.hidden_width = self.hidden.shape[0], self.hidden.shape[2]
        self.rows = self.sources * self.half
        self.part = self.width // self.replicas
        self.cuts = column_cuts(self.hidden_width, CUTS)
        self.groups = [part for part, size in enumerate(GROUPS) for _ in range(size)]

    def __call__(self, name, at=None):
        key = name if at is None else name + str(at)
        if key not in self.made:
            made = getattr(self, name)
            self.made[key] = made() if at is None else made(at)
        return self.made[key]

    def free(self, value, key):
        others = []
        for other in ORDER.get(key, ()):
            name = other.rstrip("0123456789")
            others.append(self(name, int(other[len(name) :])) if name != other else self(name))
        return after(value, *others) if others else value

    def T(self, step):
        return self.free(self("T", step - 1) if step else jnp.zeros((8, 128), jnp.float32), "T" + str(step))

    def spans(self, group):
        parts = [cut for cut, owner in zip(self.cuts, self.groups) if owner == group]
        return parts[0][0], parts[-1][1]

    def G(self):
        return shifted(self.free(self.args[1], "G"), "pipe", 1)

    def H(self):
        return shifted(self.free(self.args[2], "H"), "pipe", 1)

    def P(self, pair):
        value = jnp.stack([self("Z", 2 * pair) if pair else self("share", 0), self("Z", 2 * pair + 1)])
        return shifted(self.free(value, "P" + str(pair)), "pipe", -1)

    def picks(self):
        f32, half, tokens = jnp.float32, self.half, self.tokens
        routes = self("H")[0, :, 0]
        index = lax.broadcasted_iota(jnp.int32, (tokens, tokens), 0)
        other = lax.broadcasted_iota(jnp.int32, (tokens, tokens), 1)
        earlier = (index < other) & (routes[:, None] == routes[None, :])
        slot = jnp.sum(earlier.astype(jnp.int32), axis=0)
        row = lax.broadcasted_iota(jnp.int32, (half, tokens), 0)

        def of(column):
            place = jnp.where(routes == column, slot, tokens - 1 - slot)
            return (row == place[None, :]).astype(jnp.bfloat16)

        return of

    def scaled(self):
        rows, gates = self.free(self.args[0][0], "scaled"), self.free(self("G")[0], "scaled")
        return (gates[:, None] * rows.astype(jnp.float32)).astype(jnp.bfloat16)

    def kept(self):
        return jnp.dot(
            self("picks")(self.expert), self("scaled"), preferred_element_type=jnp.float32
        ).astype(jnp.bfloat16)

    def sent(self):
        return jnp.dot(
            self("picks")(1 - self.expert), self("scaled"), preferred_element_type=jnp.float32
        ).astype(jnp.bfloat16)

    def X(self):
        return crossed(self.free(self("sent"), "X"), "expert", 2)

    def pair(self):
        kept, came, first = self("kept"), self.free(self("X"), "pair"), self.expert == 0
        return jnp.stack([jnp.where(first, kept, came), jnp.where(first, came, kept)])

    def share(self, mask):
        return lax.dynamic_slice_in_dim(self("pair"), (self.replica ^ mask) * self.part, self.part, axis=2)

    def Z(self, mask):
        return crossed(self.free(self("share", mask), "Z" + str(mask)), "dp", mask)

    def K(self, pair):
        return crossed(self.free(self("P", pair), "K" + str(pair)), "expert", 1)

    def both(self):
        first, inner = self.core == 0, self.inner
        grads = []
        for pair in (0, 1):
            mine, theirs = self("P", pair), self.free(self("K", pair), "both")
            grads.append(jnp.stack([jnp.where(first, mine, theirs), jnp.where(first, theirs, mine)], axis=2))
        grads[1] = jnp.where(inner, grads[1][::-1], grads[1])
        grads = jnp.concatenate(grads).reshape(self.replicas, self.sources, self.half, self.part)
        places = jnp.arange(self.half, dtype=jnp.bfloat16)[None, None, :]
        ours = (places < self("lengths")[:, :, None])[..., None]
        both = jnp.concatenate([jnp.where(ours, grads, 0), jnp.where(ours, 0, grads)], axis=3)
        return both.reshape(4 * self.rows, 2 * self.part)

    def N(self, mask):
        return crossed(self.free(self.args[2], "N" + str(mask)), "expert", mask)

    def counts(self):
        routes = jnp.stack([self.args[2][0, :, 0]] + [self("N", mask)[0, :, 0] for mask in (1, 2, 3)])
        zeros = jnp.sum((after(routes) == 0).astype(jnp.float32), axis=1)
        masks = jnp.arange(self.sources)
        mine = (self.shard ^ masks)[:, None] == masks[None, :]
        counts = jnp.sum(jnp.where(mine, zeros[:, None], 0.0), axis=0)
        return jnp.where(self.expert == 0, counts, self.tokens - counts)

    def upper(self, group):
        low, high = self.spans(group)
        return after(self.hidden[:, self.half :, low:high])

    def S(self, group):
        return crossed(self.free(self("upper", group), "S" + str(group)), "expert", 2)

    def own(self, group):
        low, high = self.spans(group)
        spill = self.free(self("S", group), "own" + str(group))
        places = jnp.arange(self.half)
        mirror = (places[:, None] + places[None, :] == self.half - 1).astype(jnp.bfloat16)
        turned = jnp.einsum("cs,isk->ick", mirror, spill, preferred_element_type=jnp.float32)
        keep = places.astype(jnp.float32)[None, :] < self("counts")[:, None]
        own = jnp.where(keep[:, :, None], self.hidden[:, : self.half, low:high], turned.astype(jnp.bfloat16))
        own = own.reshape(self.rows, high - low)
        if group == 0:
            label = jnp.repeat(self("counts"), 16 // self.sources)[:, None]
            own = jnp.concatenate([own, jnp.broadcast_to(label, (16, high)).astype(jnp.bfloat16)], axis=0)
        return own

    def A(self, group):
        return crossed(self.free(self("own", group), "A" + str(group)), "dp", 1)

    def cut(self, name, part):
        group = self.groups[part]
        start = self.spans(group)[0]
        low, high = self.cuts[part]
        return self(name, group)[:, low - start : high - start]

    def couple(self, part):
        first = self.free(self.cut("A", part), "couple" + str(part))
        return jnp.concatenate([self.cut("own", part), first], axis=0)

    def M(self, part):
        return lax.ppermute(self.free(self("couple", part), "M" + str(part)), "dp", [(1, 2), (2, 1)])

    def F(self, part):
        return lax.ppermute(self.free(self("M", part), "F" + str(part)), "dp", [(2, 3), (1, 0)])

    def block(self, part):
        far = jnp.where(self.inner, self("M", part), self("F", part))
        return jnp.concatenate([self.cut("own", part), self.cut("A", part), far], axis=0)

    def lengths(self):
        return self("block", 0).reshape(4, self.rows + 16, -1)[:, self.rows :: 16 // self.sources, 0]

    def total(self, part):
        block = self.free(self("block", part), "total" + str(part))
        if self.groups[part] == 0:
            block = block.reshape(4, self.rows + 16, -1)[:, : self.rows].reshape(4 * self.rows, -1)
        return lax.dot_general(
            self("both"), block, (((0,), (0,)), ((), ())), preferred_element_type=jnp.float32
        )

    def R(self, part):
        given = self("total", part)[self.part :].astype(jnp.bfloat16)
        return crossed(self.free(given, "R" + str(part)), "expert", 2)

    def out(self):
        out = jnp.zeros((self.part, self.hidden_width), jnp.bfloat16)
        for part, (low, high) in enumerate(self.cuts):
            value = self("total", part)[: self.part] + self("R", part).astype(jnp.float32)
            out = lax.dynamic_update_slice(out, value.astype(jnp.bfloat16), (0, low))
        return out[None]


def pair_body(*args):
    return Plan(*args)("out")


def solution(mesh):
    in_specs = (
        P("pipe", ("dp", "expert"), None),
        P("pipe", ("dp", "expert")),
        P("pipe", ("dp", "expert"), None),
        P("pipe", "dp", None, None, "expert"),
    )
    out_specs = P("pipe", "dp", "expert")

    def run(input_grad, gate_prob, expert_route, saved_hidden):
        devices = mesh.shape["dp"] * mesh.shape["expert"]
        tokens = input_grad.shape[1] // devices
        pairs = mesh.shape["expert"] == 4 and mesh.shape["dp"] == 4
        body = pair_body if pairs and saved_hidden.shape[3] == tokens else general_body
        return jax.shard_map(body, mesh=mesh, in_specs=in_specs, out_specs=out_specs, check_vma=False)(
            input_grad, gate_prob, expert_route, saved_hidden
        )

    return run
```

```python
import jax
import jax.numpy as jnp
from jax import lax
from jax.sharding import PartitionSpec as P

CUTS = (2, 3, 3, 3)
GROUPS = (1, 1, 1, 1)
FIRST = ("M2",)
ORDER = {
    "F1": ("F0",),
    "F2": ("F0",),
    "F3": ("F1",),
    "M1": ("M0",),
    "M2": ("M1",),
    "M3": ("M2",),
    "N1": ("G", "H"),
    "N2": ("H",),
    "N3": ("G", "H"),
    "S1": ("sent",),
    "S2": ("S0",),
    "S3": ("Z1",),
    "T0": ("upper0",),
    "total2": ("total1",),
}


def shifted(value, axis, steps):
    count = lax.axis_size(axis)
    pairs = [(source, (source + steps) % count) for source in range(count)]
    return lax.ppermute(value, axis, pairs)


def crossed(value, axis, mask):
    pairs = [(source, source ^ mask) for source in range(lax.axis_size(axis))]
    return lax.ppermute(value, axis, pairs)


def general_body(input_grad, gate_prob, expert_route, saved_hidden):
    grad_rows = shifted(input_grad, "pipe", -1)[0]
    flight_count = lax.axis_size("expert") // 2
    capacity = saved_hidden.shape[3]
    token_count = grad_rows.shape[0]
    model_width = grad_rows.shape[1]
    routes = expert_route[0, :, 0]
    one_hot = (routes[:, None] == jnp.arange(flight_count, dtype=jnp.int32)[None, :]).astype(
        jnp.float32
    )
    row_ids = lax.broadcasted_iota(jnp.int32, (token_count, token_count), 0)
    column_ids = lax.broadcasted_iota(jnp.int32, (token_count, token_count), 1)
    earlier_mask = (column_ids < row_ids).astype(jnp.float32)
    before = jnp.dot(earlier_mask, one_hot, precision=lax.Precision.HIGHEST)
    position = jnp.sum(before * one_hot, axis=1)
    slot_values = jnp.arange(capacity, dtype=jnp.float32)
    slot_hit = one_hot[:, :, None] * (position[:, None, None] == slot_values[None, None, :]).astype(
        jnp.float32
    )
    scaled = (gate_prob[0][:, None] * grad_rows.astype(jnp.float32)).astype(jnp.bfloat16)
    outgoing = jnp.einsum(
        "tec,td->ecd", slot_hit.astype(jnp.bfloat16), scaled, preferred_element_type=jnp.float32
    ).astype(jnp.bfloat16)
    halves = outgoing.reshape(2 * flight_count, capacity // 2, model_width)
    owned_rows = lax.all_to_all(halves, "expert", split_axis=0, concat_axis=0, tiled=True)
    partner_rows = crossed(owned_rows, "expert", 1)
    parity = lax.axis_index("expert") % 2
    first_half = jnp.where(parity == 0, owned_rows, partner_rows)
    second_half = jnp.where(parity == 0, partner_rows, owned_rows)
    received = jnp.concatenate([first_half, second_half], axis=1)
    source_count = received.shape[0]
    flat_rows = received.reshape(source_count * capacity, model_width)
    hidden = saved_hidden.reshape(source_count * capacity, saved_hidden.shape[4])
    summed = lax.psum_scatter(
        lax.dot_general(
            flat_rows, hidden, (((0,), (0,)), ((), ())), preferred_element_type=jnp.float32
        ).astype(jnp.bfloat16),
        "dp",
        scatter_dimension=0,
        tiled=True,
    )
    return summed[None]


def column_cuts(width, weights):
    tiles, whole = width // 128, sum(weights)
    edges = [128 * ((tiles * sum(weights[:part])) // whole) for part in range(len(weights))] + [width]
    return list(zip(edges[:-1], edges[1:]))


def after(value, *others):
    return lax.optimization_barrier((value, *others))[0]


class Plan:
    def __init__(self, input_grad, gate_prob, expert_route, saved_hidden):
        self.made = {}
        self.args = input_grad, gate_prob, expert_route
        self.replica, self.shard = lax.axis_index("dp"), lax.axis_index("expert")
        self.replicas, self.shards = lax.axis_size("dp"), lax.axis_size("expert")
        self.expert, self.core = self.shard // 2, self.shard % 2
        self.inner = (self.replica == 1) | (self.replica == 2)
        self.tokens, self.width = input_grad.shape[1:]
        self.half = self.tokens // 2
        self.hidden = saved_hidden[0, 0]
        self.sources, self.hidden_width = self.hidden.shape[0], self.hidden.shape[2]
        self.rows = self.sources * self.half
        self.part = self.width // self.replicas
        self.cuts = column_cuts(self.hidden_width, CUTS)
        self.groups = [part for part, size in enumerate(GROUPS) for _ in range(size)]

    def __call__(self, name, at=None):
        key = name if at is None else name + str(at)
        if key not in self.made:
            made = getattr(self, name)
            self.made[key] = made() if at is None else made(at)
        return self.made[key]

    def free(self, value, key):
        others = []
        for other in ORDER.get(key, ()):
            name = other.rstrip("0123456789")
            others.append(self(name, int(other[len(name) :])) if name != other else self(name))
        return after(value, *others) if others else value

    def T(self, step):
        return self.free(self("T", step - 1) if step else jnp.zeros((8, 128), jnp.float32), "T" + str(step))

    def spans(self, group):
        parts = [cut for cut, owner in zip(self.cuts, self.groups) if owner == group]
        return parts[0][0], parts[-1][1]

    def G(self):
        return shifted(self.free(self.args[1], "G"), "pipe", 1)

    def H(self):
        return shifted(self.free(self.args[2], "H"), "pipe", 1)

    def pick(self):
        half, tokens = self.half, self.tokens
        routes = self("H")[0, :, 0]
        index = lax.broadcasted_iota(jnp.int32, (tokens, tokens), 0)
        other = lax.broadcasted_iota(jnp.int32, (tokens, tokens), 1)
        earlier = (index < other) & (routes[:, None] == routes[None, :])
        slot = jnp.sum(earlier.astype(jnp.int32), axis=0)
        place = jnp.where(routes == self.expert, slot, tokens - 1 - slot)
        place = jnp.where(place < half, place, tokens + half - 1 - place)
        return (index == place[None, :]).astype(jnp.bfloat16)

    def scaled(self):
        rows, gates = self.free(self.args[0][0], "scaled"), self.free(self("G")[0], "scaled")
        return (gates[:, None] * rows.astype(jnp.float32)).astype(jnp.bfloat16)

    def sent(self):
        rows = jnp.dot(self("pick"), self("scaled"), preferred_element_type=jnp.float32)
        return rows.astype(jnp.bfloat16).reshape(2, self.half, self.width)

    def share(self, mask):
        return lax.dynamic_slice_in_dim(self("sent"), (self.replica ^ mask) * self.part, self.part, axis=2)

    def Z(self, mask):
        return crossed(self.free(self("share", mask), "Z" + str(mask)), "dp", mask)

    def near(self):
        at = [self("share", 0)] + [self("Z", mask) for mask in (1, 2, 3)]
        at[1] = self.free(at[1], "near")
        at[2], at[3] = jnp.where(self.inner, at[3], at[2]), jnp.where(self.inner, at[2], at[3])
        return jnp.stack(at, axis=1)

    def X(self):
        return crossed(self.free(self("near")[1], "X"), "expert", 2)

    def pair(self):
        kept, came, first = self("near")[0], self.free(self("X"), "pair"), self.expert == 0
        return jnp.stack([jnp.where(first, kept, came), jnp.where(first, came, kept)], axis=1)

    def P(self):
        return shifted(self.free(self("pair"), "P"), "pipe", -1)

    def K(self):
        return crossed(self.free(self("P"), "K"), "expert", 1)

    def both(self):
        mine, theirs, first = self("P"), self.free(self("K"), "both"), self.core == 0
        grads = jnp.stack([jnp.where(first, mine, theirs), jnp.where(first, theirs, mine)], axis=2)
        grads = grads.reshape(self.replicas, self.sources, self.half, self.part)
        places = jnp.arange(self.half, dtype=jnp.bfloat16)[None, None, :]
        ours = (places < self("lengths")[:, :, None])[..., None]
        both = jnp.concatenate([jnp.where(ours, grads, 0), jnp.where(ours, 0, grads)], axis=3)
        return both.reshape(4 * self.rows, 2 * self.part)

    def N(self, mask):
        return crossed(self.free(self.args[2], "N" + str(mask)), "expert", mask)

    def counts(self):
        routes = jnp.stack([self.args[2][0, :, 0]] + [self("N", mask)[0, :, 0] for mask in (1, 2, 3)])
        zeros = jnp.sum((after(routes) == 0).astype(jnp.float32), axis=1)
        masks = jnp.arange(self.sources)
        mine = (self.shard ^ masks)[:, None] == masks[None, :]
        counts = jnp.sum(jnp.where(mine, zeros[:, None], 0.0), axis=0)
        return jnp.where(self.expert == 0, counts, self.tokens - counts)

    def upper(self, group):
        low, high = self.spans(group)
        return after(self.hidden[:, self.half :, low:high])

    def S(self, group):
        return crossed(self.free(self("upper", group), "S" + str(group)), "expert", 2)

    def own(self, group):
        low, high = self.spans(group)
        spill = self.free(self("S", group), "own" + str(group))
        places = jnp.arange(self.half)
        mirror = (places[:, None] + places[None, :] == self.half - 1).astype(jnp.bfloat16)
        turned = jnp.einsum("cs,isk->ick", mirror, spill, preferred_element_type=jnp.float32)
        keep = places.astype(jnp.float32)[None, :] < self("counts")[:, None]
        own = jnp.where(keep[:, :, None], self.hidden[:, : self.half, low:high], turned.astype(jnp.bfloat16))
        own = own.reshape(self.rows, high - low)
        if group == 0:
            label = jnp.repeat(self("counts"), 16 // self.sources)[:, None]
            own = jnp.concatenate([own, jnp.broadcast_to(label, (16, high)).astype(jnp.bfloat16)], axis=0)
        return own

    def A(self, group):
        return crossed(self.free(self("own", group), "A" + str(group)), "dp", 1)

    def cut(self, name, part):
        group = self.groups[part]
        start = self.spans(group)[0]
        low, high = self.cuts[part]
        return self(name, group)[:, low - start : high - start]

    def couple(self, part):
        first = self.free(self.cut("A", part), "couple" + str(part))
        return jnp.concatenate([self.cut("own", part), first], axis=0)

    def M(self, part):
        return lax.ppermute(self.free(self("couple", part), "M" + str(part)), "dp", [(1, 2), (2, 1)])

    def F(self, part):
        return lax.ppermute(self.free(self("M", part), "F" + str(part)), "dp", [(0, 1), (1, 0), (2, 3), (3, 2)])

    def block(self, part):
        far = jnp.where(self.inner, self("M", part), self("F", part))
        return jnp.concatenate([self.cut("own", part), self.cut("A", part), far], axis=0)

    def lengths(self):
        return self("block", 0).reshape(4, self.rows + 16, -1)[:, self.rows :: 16 // self.sources, 0]

    def total(self, part):
        block = self.free(self("block", part), "total" + str(part))
        if self.groups[part] == 0:
            block = block.reshape(4, self.rows + 16, -1)[:, : self.rows].reshape(4 * self.rows, -1)
        return lax.dot_general(
            self("both"), block, (((0,), (0,)), ((), ())), preferred_element_type=jnp.float32
        )

    def R(self, part):
        given = self("total", part)[self.part :].astype(jnp.bfloat16)
        return crossed(self.free(given, "R" + str(part)), "expert", 2)

    def out(self):
        out = jnp.zeros((self.part, self.hidden_width), jnp.bfloat16)
        for part, (low, high) in enumerate(self.cuts):
            value = self("total", part)[: self.part] + self("R", part).astype(jnp.float32)
            out = lax.dynamic_update_slice(out, value.astype(jnp.bfloat16), (0, low))
        return out[None]


def pair_body(*args):
    plan = Plan(*args)
    for name in FIRST:
        kind = name.rstrip("0123456789")
        plan(kind, int(name[len(kind) :])) if kind != name else plan(name)
    return plan("out")


def solution(mesh):
    in_specs = (
        P("pipe", ("dp", "expert"), None),
        P("pipe", ("dp", "expert")),
        P("pipe", ("dp", "expert"), None),
        P("pipe", "dp", None, None, "expert"),
    )
    out_specs = P("pipe", "dp", "expert")

    def run(input_grad, gate_prob, expert_route, saved_hidden):
        devices = mesh.shape["dp"] * mesh.shape["expert"]
        tokens = input_grad.shape[1] // devices
        pairs = mesh.shape["expert"] == 4 and mesh.shape["dp"] == 4
        body = pair_body if pairs and saved_hidden.shape[3] == tokens else general_body
        return jax.shard_map(body, mesh=mesh, in_specs=in_specs, out_specs=out_specs, check_vma=False)(
            input_grad, gate_prob, expert_route, saved_hidden
        )

    return run
```

```python
import jax
import jax.numpy as jnp
from jax import lax
from jax.sharding import PartitionSpec as P

CUTS = (2, 3, 3, 3)
GROUPS = (1, 1, 1, 1)
FIRST = ("M2",)
ORDER = {
    "F1": ("F0",),
    "F2": ("F0",),
    "F3": ("F1",),
    "M1": ("M0",),
    "M2": ("M1",),
    "M3": ("M2",),
    "N1": ("G", "H"),
    "N2": ("H",),
    "N3": ("G", "H"),
    "S1": ("sent",),
    "S2": ("S0",),
    "S3": ("Z1",),
    "T0": ("upper0",),
    "total2": ("total1",),
}


def shifted(value, axis, steps):
    count = lax.axis_size(axis)
    pairs = [(source, (source + steps) % count) for source in range(count)]
    return lax.ppermute(value, axis, pairs)


def crossed(value, axis, mask):
    pairs = [(source, source ^ mask) for source in range(lax.axis_size(axis))]
    return lax.ppermute(value, axis, pairs)


def general_body(input_grad, gate_prob, expert_route, saved_hidden):
    grad_rows = shifted(input_grad, "pipe", -1)[0]
    flight_count = lax.axis_size("expert") // 2
    capacity = saved_hidden.shape[3]
    token_count = grad_rows.shape[0]
    model_width = grad_rows.shape[1]
    routes = expert_route[0, :, 0]
    one_hot = (routes[:, None] == jnp.arange(flight_count, dtype=jnp.int32)[None, :]).astype(
        jnp.float32
    )
    row_ids = lax.broadcasted_iota(jnp.int32, (token_count, token_count), 0)
    column_ids = lax.broadcasted_iota(jnp.int32, (token_count, token_count), 1)
    earlier_mask = (column_ids < row_ids).astype(jnp.float32)
    before = jnp.dot(earlier_mask, one_hot, precision=lax.Precision.HIGHEST)
    position = jnp.sum(before * one_hot, axis=1)
    slot_values = jnp.arange(capacity, dtype=jnp.float32)
    slot_hit = one_hot[:, :, None] * (position[:, None, None] == slot_values[None, None, :]).astype(
        jnp.float32
    )
    scaled = (gate_prob[0][:, None] * grad_rows.astype(jnp.float32)).astype(jnp.bfloat16)
    outgoing = jnp.einsum(
        "tec,td->ecd", slot_hit.astype(jnp.bfloat16), scaled, preferred_element_type=jnp.float32
    ).astype(jnp.bfloat16)
    halves = outgoing.reshape(2 * flight_count, capacity // 2, model_width)
    owned_rows = lax.all_to_all(halves, "expert", split_axis=0, concat_axis=0, tiled=True)
    partner_rows = crossed(owned_rows, "expert", 1)
    parity = lax.axis_index("expert") % 2
    first_half = jnp.where(parity == 0, owned_rows, partner_rows)
    second_half = jnp.where(parity == 0, partner_rows, owned_rows)
    received = jnp.concatenate([first_half, second_half], axis=1)
    source_count = received.shape[0]
    flat_rows = received.reshape(source_count * capacity, model_width)
    hidden = saved_hidden.reshape(source_count * capacity, saved_hidden.shape[4])
    summed = lax.psum_scatter(
        lax.dot_general(
            flat_rows, hidden, (((0,), (0,)), ((), ())), preferred_element_type=jnp.float32
        ).astype(jnp.bfloat16),
        "dp",
        scatter_dimension=0,
        tiled=True,
    )
    return summed[None]


def column_cuts(width, weights):
    tiles, whole = width // 128, sum(weights)
    edges = [128 * ((tiles * sum(weights[:part])) // whole) for part in range(len(weights))] + [width]
    return list(zip(edges[:-1], edges[1:]))


def after(value, *others):
    return lax.optimization_barrier((value, *others))[0]


class Plan:
    def __init__(self, input_grad, gate_prob, expert_route, saved_hidden):
        self.made = {}
        self.args = input_grad, gate_prob, expert_route
        self.replica, self.shard = lax.axis_index("dp"), lax.axis_index("expert")
        self.replicas, self.shards = lax.axis_size("dp"), lax.axis_size("expert")
        self.expert, self.core = self.shard // 2, self.shard % 2
        self.inner = (self.replica == 1) | (self.replica == 2)
        self.tokens, self.width = input_grad.shape[1:]
        self.half = self.tokens // 2
        self.hidden = saved_hidden[0, 0]
        self.sources, self.hidden_width = self.hidden.shape[0], self.hidden.shape[2]
        self.rows = self.sources * self.half
        self.part = self.width // self.replicas
        self.cuts = column_cuts(self.hidden_width, CUTS)
        self.groups = [part for part, size in enumerate(GROUPS) for _ in range(size)]

    def __call__(self, name, at=None):
        key = name if at is None else name + str(at)
        if key not in self.made:
            made = getattr(self, name)
            self.made[key] = made() if at is None else made(at)
        return self.made[key]

    def free(self, value, key):
        others = []
        for other in ORDER.get(key, ()):
            name = other.rstrip("0123456789")
            others.append(self(name, int(other[len(name) :])) if name != other else self(name))
        return after(value, *others) if others else value

    def T(self, step):
        return self.free(self("T", step - 1) if step else jnp.zeros((8, 128), jnp.float32), "T" + str(step))

    def spans(self, group):
        parts = [cut for cut, owner in zip(self.cuts, self.groups) if owner == group]
        return parts[0][0], parts[-1][1]

    def G(self):
        return shifted(self.free(self.args[1], "G"), "pipe", 1)

    def H(self):
        return shifted(self.free(self.args[2], "H"), "pipe", 1)

    def pick(self):
        half, tokens = self.half, self.tokens
        routes = self("H")[0, :, 0]
        index = lax.broadcasted_iota(jnp.int32, (tokens, tokens), 0)
        other = lax.broadcasted_iota(jnp.int32, (tokens, tokens), 1)
        earlier = (index < other) & (routes[:, None] == routes[None, :])
        slot = jnp.sum(earlier.astype(jnp.int32), axis=0)
        place = jnp.where(routes == self.expert, slot, tokens - 1 - slot)
        place = jnp.where(place < half, place, tokens + half - 1 - place)
        return (index == place[None, :]).astype(jnp.bfloat16)

    def scaled(self):
        rows, gates = self.free(self.args[0][0], "scaled"), self.free(self("G")[0], "scaled")
        return (gates[:, None] * rows.astype(jnp.float32)).astype(jnp.bfloat16)

    def sent(self):
        rows = jnp.dot(self("pick"), self("scaled"), preferred_element_type=jnp.float32)
        return rows.astype(jnp.bfloat16).reshape(2, self.half, self.width)

    def share(self, mask):
        return lax.dynamic_slice_in_dim(self("sent"), (self.replica ^ mask) * self.part, self.part, axis=2)

    def Z(self, mask):
        return crossed(self.free(self("share", mask), "Z" + str(mask)), "dp", mask)

    def near(self):
        at = [self("share", 0)] + [self("Z", mask) for mask in (1, 2, 3)]
        at[1] = self.free(at[1], "near")
        at[2], at[3] = jnp.where(self.inner, at[3], at[2]), jnp.where(self.inner, at[2], at[3])
        return jnp.stack(at, axis=1)

    def X(self):
        return crossed(self.free(self("near")[1], "X"), "expert", 2)

    def pair(self):
        kept, came, first = self("near")[0], self.free(self("X"), "pair"), self.expert == 0
        return jnp.stack([jnp.where(first, kept, came), jnp.where(first, came, kept)], axis=1)

    def P(self):
        return shifted(self.free(self("pair"), "P"), "pipe", -1)

    def K(self):
        return crossed(self.free(self("P"), "K"), "expert", 1)

    def both(self):
        mine, theirs, first = self("P"), self.free(self("K"), "both"), self.core == 0
        grads = jnp.stack([jnp.where(first, mine, theirs), jnp.where(first, theirs, mine)], axis=2)
        grads = grads.reshape(self.replicas, self.sources, self.half, self.part)
        places = jnp.arange(self.half, dtype=jnp.bfloat16)[None, None, :]
        ours = (places < self("lengths")[:, :, None])[..., None]
        both = jnp.concatenate([jnp.where(ours, grads, 0), jnp.where(ours, 0, grads)], axis=3)
        return both.reshape(4 * self.rows, 2 * self.part)

    def N(self, mask):
        return crossed(self.free(self.args[2], "N" + str(mask)), "expert", mask)

    def counts(self):
        routes = jnp.stack([self.args[2][0, :, 0]] + [self("N", mask)[0, :, 0] for mask in (1, 2, 3)])
        zeros = jnp.sum((after(routes) == 0).astype(jnp.float32), axis=1)
        masks = jnp.arange(self.sources)
        mine = (self.shard ^ masks)[:, None] == masks[None, :]
        counts = jnp.sum(jnp.where(mine, zeros[:, None], 0.0), axis=0)
        return jnp.where(self.expert == 0, counts, self.tokens - counts)

    def upper(self, group):
        low, high = self.spans(group)
        return after(self.hidden[:, self.half :, low:high])

    def S(self, group):
        return crossed(self.free(self("upper", group), "S" + str(group)), "expert", 2)

    def own(self, group):
        low, high = self.spans(group)
        spill = self.free(self("S", group), "own" + str(group))
        places = jnp.arange(self.half)
        mirror = (places[:, None] + places[None, :] == self.half - 1).astype(jnp.bfloat16)
        turned = jnp.einsum("cs,isk->ick", mirror, spill, preferred_element_type=jnp.float32)
        keep = places.astype(jnp.float32)[None, :] < self("counts")[:, None]
        own = jnp.where(keep[:, :, None], self.hidden[:, : self.half, low:high], turned.astype(jnp.bfloat16))
        own = own.reshape(self.rows, high - low)
        if group == 0:
            label = jnp.repeat(self("counts"), 16 // self.sources)[:, None]
            own = jnp.concatenate([own, jnp.broadcast_to(label, (16, high)).astype(jnp.bfloat16)], axis=0)
        return own

    def A(self, group):
        return crossed(self.free(self("own", group), "A" + str(group)), "dp", 1)

    def cut(self, name, part):
        group = self.groups[part]
        start = self.spans(group)[0]
        low, high = self.cuts[part]
        return self(name, group)[:, low - start : high - start]

    def couple(self, part):
        first = self.free(self.cut("A", part), "couple" + str(part))
        return jnp.concatenate([self.cut("own", part), first], axis=0)

    def M(self, part):
        return lax.ppermute(self.free(self("couple", part), "M" + str(part)), "dp", [(1, 2), (2, 1)])

    def F(self, part):
        return lax.ppermute(self.free(self("M", part), "F" + str(part)), "dp", [(2, 3), (1, 0)] + ([(0, 1), (3, 2)] if part in (0, 2, 3) else []))

    def block(self, part):
        far = jnp.where(self.inner, self("M", part), self("F", part))
        return jnp.concatenate([self.cut("own", part), self.cut("A", part), far], axis=0)

    def lengths(self):
        return self("block", 0).reshape(4, self.rows + 16, -1)[:, self.rows :: 16 // self.sources, 0]

    def total(self, part):
        block = self.free(self("block", part), "total" + str(part))
        if self.groups[part] == 0:
            block = block.reshape(4, self.rows + 16, -1)[:, : self.rows].reshape(4 * self.rows, -1)
        return lax.dot_general(
            self("both"), block, (((0,), (0,)), ((), ())), preferred_element_type=jnp.float32
        )

    def R(self, part):
        given = self("total", part)[self.part :].astype(jnp.bfloat16)
        return crossed(self.free(given, "R" + str(part)), "expert", 2)

    def out(self):
        out = jnp.zeros((self.part, self.hidden_width), jnp.bfloat16)
        for part, (low, high) in enumerate(self.cuts):
            value = self("total", part)[: self.part] + self("R", part).astype(jnp.float32)
            out = lax.dynamic_update_slice(out, value.astype(jnp.bfloat16), (0, low))
        return out[None]


def pair_body(*args):
    plan = Plan(*args)
    for name in FIRST:
        kind = name.rstrip("0123456789")
        plan(kind, int(name[len(kind) :])) if kind != name else plan(name)
    return plan("out")


def solution(mesh):
    in_specs = (
        P("pipe", ("dp", "expert"), None),
        P("pipe", ("dp", "expert")),
        P("pipe", ("dp", "expert"), None),
        P("pipe", "dp", None, None, "expert"),
    )
    out_specs = P("pipe", "dp", "expert")

    def run(input_grad, gate_prob, expert_route, saved_hidden):
        devices = mesh.shape["dp"] * mesh.shape["expert"]
        tokens = input_grad.shape[1] // devices
        pairs = mesh.shape["expert"] == 4 and mesh.shape["dp"] == 4
        body = pair_body if pairs and saved_hidden.shape[3] == tokens else general_body
        return jax.shard_map(body, mesh=mesh, in_specs=in_specs, out_specs=out_specs, check_vma=False)(
            input_grad, gate_prob, expert_route, saved_hidden
        )

    return run
```
